128 devices in a mesh: grp: 8 (over y, core), dev: 16 (over x, z).
Axes of the slice: x: 4, y: 4, z: 4, core: 2. Of those that a mesh axis runs over, the one named last changes fastest.
Arguments:
- latent: bfloat16 [8192, 128, 512], P('grp', 'dev'), may hold values from -6 to 6
- value_up: bfloat16 [128, 512, 128], P('dev'), may hold values from -0.25 to 0.25
- out_proj: bfloat16 [16384, 7168], P('dev'), may hold values from -0.0625 to 0.0625
- adapter_down: bfloat16 [32, 256, 16384], P('grp', None, 'dev'), may hold values from -0.046875 to 0.046875
- adapter_up: bfloat16 [32, 256, 7168], P('grp', None, 'dev'), may hold values from -0.375 to 0.375
- pair_ids: int32 [32, 2], P('grp'), may hold values from 0 to 31, as said below
- mix_weights: float32 [2, 8192], P(None, 'grp'), may hold values from 0.25 to 1
Outputs:
- projected: bfloat16 [8192, 7168], P('grp', 'dev')
The draws below stay inside these ranges and needn't reach their ends.
Inputs may be any that keep to these rules, and one draw needn't show every extreme that they name: `pair_ids`: adapter a belongs to index a // 4 of grp. Among the 8 adapter picks of the blocks of one index of grp, at most 2 name adapters of one index of grp, and in every index of grp some index of grp receives exactly 2. The two adapters of a block differ.
All inputs are finite; a program needn't handle non-finite values.
Results may differ from the reference program's by a relative error of at most 0.02.
Values may be sent and summed in bfloat16 or wider, within the bound.
A program may use at most 192 MiB of HBM per device.

```python
import jax
import jax.numpy as jnp
from jax import lax

MODEL_WIDTH = 7168
HEADS = 128
VDIM = 128
LAT = 512
RANK = 256
BLOCK = 256
ADP_OWN = 4
CAP = 2
ROWS_GRP = 1024
HID = 16384
ADAPTERS = 32
ROWS = 8192
NBLK = 32
N_DEV = 16


def draw_pair_ids(key, part):
    key = jax.random.fold_in(key, 7)
    owner_count = ADAPTERS // ADP_OWN
    per_group = ROWS_GRP // BLOCK
    picks = 2 * per_group
    group_count = NBLK // per_group
    pool = jnp.repeat(jnp.arange(owner_count, dtype=jnp.int32), CAP)
    pool_size = owner_count * CAP

    def one_group(sub):
        key_hot, key_pool, key_order, key_first, key_second = jax.random.split(sub, 5)
        hot = jax.random.randint(key_hot, (), 0, owner_count, dtype=jnp.int32)
        ranks = jax.random.permutation(key_pool, pool_size).astype(jnp.int32)
        scores = jnp.where(pool == hot, ranks + 2 * pool_size, ranks)
        order = jnp.argsort(scores)
        others = pool[order][:picks - CAP]
        owners = jnp.concatenate([jnp.full((CAP,), hot, jnp.int32), others])
        owners = owners[jax.random.permutation(key_order, picks)]
        first = jax.random.randint(key_first, (per_group,), 0, ADP_OWN, dtype=jnp.int32)
        second = (first + jax.random.randint(key_second, (per_group,), 1, ADP_OWN, dtype=jnp.int32)) % ADP_OWN
        locals_pair = jnp.stack([first, second], axis=1)
        return owners.reshape(per_group, 2) * ADP_OWN + locals_pair
    keys = jax.random.split(key, group_count)
    return jax.vmap(one_group)(keys).reshape(NBLK, 2).astype(jnp.int32)


def spiked(entries, key, source, target, shards_of, factor):
    def block_of(dim):
        return (jnp.arange(entries.shape[dim]) // (entries.shape[dim] // shards_of)).reshape((-1,) + (1,) * (entries.ndim - 1 - dim))

    near = jax.random.permutation(key, shards_of)[block_of(target)]
    far = (block_of(target) + shards_of // 2) % shards_of
    return jnp.where((block_of(source) == near) | (block_of(source) == far), factor * entries, entries)


def steps_of(stream_key, shape, shards, smallest, largest):
    gain, own = 1.0, jax.random.fold_in(stream_key, 6)
    for dim, parts in shards:
        heights = jnp.exp(jax.random.uniform(jax.random.fold_in(own, dim), (parts,), jnp.float32, smallest / len(shards), largest / len(shards)))
        gain = gain * jnp.repeat(heights, shape[dim] // parts).reshape([-1 if axis == dim else 1 for axis in range(len(shape))])
    return gain


def bell_draw(key, extent, width, limit, cuts=(), kind=jnp.bfloat16):
    result = width * jax.random.normal(key, extent, jnp.float32)
    if cuts:
        result = result * steps_of(key, extent, cuts, -0.22, 0.18)
    return jnp.clip(result, -limit, limit).astype(kind)


def gaussian_with(rng, extent, width, most, cuts, heavy, held_as=jnp.bfloat16):
    values = width * jax.random.normal(rng, extent, jnp.float32)
    if cuts:
        values = values * steps_of(rng, extent, cuts, -0.22, 0.18)
    return jnp.clip(spiked(values, jax.random.fold_in(rng, 3), *heavy), -most, most).astype(held_as)


def setup_inputs(seed: int = 0) -> dict:
    streams_of = jax.random.split(jax.random.key(seed), 8)
    return {
        "latent": bell_draw(streams_of[0], (ROWS, HEADS, LAT), 1.0, 6.0, ((0, 8), (1, 16))),
        "value_up": bell_draw(streams_of[1], (HEADS, LAT, VDIM), LAT ** -0.5, 0.25, ((0, 16),)),
        "out_proj": gaussian_with(streams_of[2], (HID, MODEL_WIDTH), HID ** -0.5, 0.0625, ((0, 16),), (0, 1, 16, 2.0)),
        "adapter_down": bell_draw(streams_of[3], (ADAPTERS, RANK, HID), HID ** -0.5, 0.046875, ((0, 8), (2, 16))),
        "adapter_up": bell_draw(streams_of[4], (ADAPTERS, RANK, MODEL_WIDTH), RANK ** -0.5, 0.375, ((0, 8), (2, 16))),
        "pair_ids": draw_pair_ids(jax.random.fold_in(streams_of[7], 71), 0),
        "mix_weights": jnp.clip(0.25 + 0.75 * jax.random.uniform(streams_of[6], (2, ROWS), jnp.float32) ** steps_of(streams_of[6], (2, ROWS), ((1, 8),), -0.2, 0.2), 0.25, 1.0),
    }


def reference(latent, value_up, out_proj, adapter_down, adapter_up, pair_ids, mix_weights):
    total_rows = latent.shape[0]
    head_group = HEADS // N_DEV
    width_group = head_group * VDIM
    pieces = []
    base_projection = jnp.zeros((total_rows, MODEL_WIDTH), jnp.float32)
    for shard in range(N_DEV):
        lat_part = latent[:, shard * head_group:(shard + 1) * head_group].astype(jnp.float32)
        up_part = value_up[shard * head_group:(shard + 1) * head_group].astype(jnp.float32)
        heads_part = jnp.einsum('rhl,hlv->rhv', lat_part, up_part).astype(jnp.bfloat16).reshape(total_rows, width_group)
        pieces.append(heads_part)
        term = jnp.dot(heads_part, out_proj[shard * width_group:(shard + 1) * width_group], preferred_element_type=jnp.float32)
        term = lax.optimization_barrier(term.astype(jnp.bfloat16)).astype(jnp.float32)
        base_projection = base_projection + term
    heads_out = jnp.concatenate(pieces, axis=1)
    row_block_count = total_rows // BLOCK

    def single_block(index):
        start = (index * BLOCK).astype(jnp.int32)
        rows_in = lax.dynamic_slice_in_dim(heads_out, start, BLOCK, 0)
        total = jnp.zeros((BLOCK, MODEL_WIDTH), jnp.float32)
        for pick in range(2):
            chosen = pair_ids[index, pick]
            low = jnp.dot(rows_in, adapter_down[chosen].T, preferred_element_type=jnp.float32).astype(jnp.bfloat16)
            lifted = jnp.dot(low, adapter_up[chosen], preferred_element_type=jnp.float32).astype(jnp.bfloat16)
            lifted = lax.optimization_barrier(lifted).astype(jnp.float32)
            weight = lax.dynamic_slice_in_dim(mix_weights[pick], start, BLOCK, 0)
            total = total + weight[:, None] * lifted
        return total

    low_rank_term = lax.map(single_block, jnp.arange(row_block_count, dtype=jnp.int32)).reshape(total_rows, MODEL_WIDTH)
    return (base_projection + low_rank_term).astype(jnp.bfloat16)
```

```python
import functools

import jax
import jax.numpy as jnp
from jax import lax
from jax.experimental import pallas as pl
from jax.experimental.pallas import tpu as pltpu
from jax.sharding import PartitionSpec as P

MESH = pl.DeviceIdType.MESH
F32 = jnp.float32
BF16 = jnp.bfloat16
CHUNKS = 7
LAG = 4
P_SLOTS = 3
S1_SLOTS = 3
S23_SLOTS = 5
R_SLOTS = 3


def roll64(x):
    return pltpu.roll(x, 64, 1)


def kernel(
    latent, value_up, out_proj, down, up_t, ids, mix, out,
    wide, vup, heads, w, p, s1r, s2r, s3r, r, t1r, t2r, t3r, f,
    gdn, gup, low, l1r, mid, l2r, lowf,
    lat_sem, vup_sem, w_sem, own_sem,
    s_send, s_recv, t_send, t_recv, y_send, y_recv, l_send, l_recv,
):
    g = lax.axis_index("grp")
    d = lax.axis_index("dev")
    y, core = g // 2, g % 2
    x, z = d // 4, d % 4

    def at(yy=None, cc=None, xx=None, zz=None):
        yy = y if yy is None else yy
        cc = core if cc is None else cc
        xx = x if xx is None else xx
        zz = z if zz is None else zz
        return (yy * 2 + cc, xx * 4 + zz)

    def off(v, k):
        return lax.rem(v + k, 4)

    y_up, y_down, sibling = at(yy=off(y, 1)), at(yy=off(y, 3)), at(cc=1 - core)
    x_at = [None] + [at(xx=off(x, k)) for k in (1, 2, 3)]
    z_at = [None] + [at(zz=off(z, k)) for k in (1, 2, 3)]

    def remote(src, dst, send, recv, to):
        return pltpu.make_async_remote_copy(
            src_ref=src, dst_ref=dst, send_sem=send, recv_sem=recv, device_id=to, device_id_type=MESH
        )

    barrier = pltpu.get_barrier_semaphore()
    for n in x_at[1:] + z_at[1:] + [y_up, y_down, sibling]:
        pl.semaphore_signal(barrier, inc=1, device_id=n, device_id_type=MESH)

    def lat_start(c, slot):
        for k in range(4):
            for m in range(4):
                pltpu.make_async_copy(
                    latent.at[pl.ds(pl.multiple_of(c * 2048 + m * 512, 512), 512), pl.ds(k * 128, 128)],
                    p.at[slot, k, m], lat_sem.at[slot]).start()

    def lat_wait(slot):
        pltpu.make_async_copy(p.at[slot], p.at[slot], lat_sem.at[slot]).wait()

    def w_start(t, slot):
        @pl.loop(0, 8)
        def _(q):
            for par in range(2):
                pltpu.make_async_copy(
                    out_proj.at[:, pl.ds(pl.multiple_of(q * 896 + par * 512 + t * 128, 128), 128)],
                    w.at[slot, q, :, pl.ds(par * 128, 128)], w_sem.at[slot]).start()

    def w_start_tail(slot):
        @pl.loop(0, 8)
        def _(q):
            pltpu.make_async_copy(
                out_proj.at[:, pl.ds(pl.multiple_of(q * 896 + 384, 128), 128)],
                w.at[slot, q, :, pl.ds(0, 128)], w_sem.at[slot]).start()

    def w_wait(slot):
        pltpu.make_async_copy(w.at[slot], w.at[slot], w_sem.at[slot]).wait()

    vup_copy = pltpu.make_async_copy(value_up, vup, vup_sem)
    vup_copy.start()
    lat_start(0, 0)
    lat_start(1, 1)
    pl.semaphore_wait(barrier, 9)

    own = g * 4

    def block(yy, cc):
        return (yy * 2 + cc) * 4

    def adapters(kind, src, gathered):
        base = kind * 16
        below, above, across = block(off(y, 3), core), block(off(y, 1), core), block(off(y, 2), core)

        def cp(k, source, unit, count, to):
            return remote(source, gathered.at[pl.ds(unit, count)], y_send.at[base + k], y_recv.at[base + k], to)

        def here(unit, count):
            return gathered.at[pl.ds(unit, count)]

        first = [
            cp(0, src.at[pl.ds(0, 2)], own, 2, y_up),
            cp(1, src.at[pl.ds(2, 2)], own + 2, 2, y_down),
            cp(2, src.at[pl.ds(2, 2)], own + 2, 2, y_up),
            cp(3, src.at[pl.ds(0, 2)], own, 2, y_down),
            cp(4, src, own, 4, sibling),
        ]
        second = [
            cp(5, here(below, 2), below, 2, y_up),
            cp(6, here(above + 2, 2), above + 2, 2, y_down),
            cp(7, here(below, 4), below, 4, sibling),
            cp(8, here(above, 4), above, 4, sibling),
        ]
        third = [
            cp(9, here(across, 2), across, 2, sibling),
            cp(10, here(across + 2, 2), across + 2, 2, sibling),
        ]
        return first, second, third

    dn1, dn2, dn3 = adapters(0, down, gdn)
    up1, up2, up3 = adapters(1, up_t, gup)

    def start(copies):
        for c in copies:
            c.start()

    def got(copies):
        for c in copies:
            c.wait_recv()

    start(dn1)
    own_dn = pltpu.make_async_copy(down, gdn.at[pl.ds(own, 4)], own_sem.at[0])
    own_up = pltpu.make_async_copy(up_t, gup.at[pl.ds(own, 4)], own_sem.at[1])
    own_dn.start()
    own_up.start()
    w_start(0, 0)
    w_start(1, 1)

    vup_copy.wait()

    @pl.loop(0, 4)
    def _(c):
        slot = lax.rem(c, 2)
        lat_wait(slot)
        for k in range(4):
            for m in range(4):
                wide[k, pl.ds(m * 512, 512), :] = p[slot, k, m].astype(F32)

        @pl.when(c < 2)
        def _():
            lat_start(c + 2, slot)

        for h in range(8):
            xh = jnp.concatenate([wide[k, pl.ds(h, 256, stride=8), :] for k in range(4)], axis=1).astype(BF16)
            heads[pl.ds(pl.multiple_of(c * 256, 256), 256), pl.ds(h * 128, 128)] = jnp.dot(
                xh, vup[h], preferred_element_type=F32).astype(BF16)

    coord = (x, z)
    ring = (x_at, z_at)

    def piece(slot, dim, dest, half):
        rows = pl.ds(dim * 256 + half * 128, 128)
        return p.at[slot, dest, :, rows, :] if dim == 0 else p.at[slot, :, dest, rows, :]

    def s_copies(c, kind):
        slot, n1, n5 = lax.rem(c, P_SLOTS), lax.rem(c, S1_SLOTS), lax.rem(c, S23_SLOTS)
        copies = []
        for dim in range(2):
            me, to = coord[dim], ring[dim]
            plus, opp, minus = off(me, 1), off(me, 2), off(me, 3)
            what = {0: ((opp, 0), (opp, 1)), 1: ((plus, 1), (minus, 0)), 2: ((plus, 0), (minus, 1))}[kind]
            land = (s1r.at[n1], s2r.at[n5], s3r.at[n5])[kind]
            for way in range(2):
                dest, half = what[way]
                copies.append(remote(
                    piece(slot, dim, dest, half), land.at[dim, way],
                    s_send.at[kind, c, dim, way], s_recv.at[kind, c, dim, way], to[1] if way == 0 else to[3]))
        return copies

    def t_copies(c, kind):
        slot = lax.rem(c, R_SLOTS)
        copies = []
        for dim in range(2):
            me, to = coord[1 - dim], ring[1 - dim]
            plus, opp, minus = off(me, 1), off(me, 2), off(me, 3)
            what = {0: ((opp, 0), (opp, 1)), 1: ((plus, 1), (minus, 0)), 2: ((plus, 0), (minus, 1))}[kind]
            land = (t1r, t2r, t3r)[kind]
            for way in range(2):
                dest, half = what[way]
                copies.append(remote(
                    r.at[slot, dim, dest, pl.ds(half * 128, 128), :], land.at[c, dim, way],
                    t_send.at[kind, c, dim, way], t_recv.at[kind, c, dim, way], to[1] if way == 0 else to[3]))
        return copies

    def produce(c):
        slot = lax.rem(c, P_SLOTS)

        @pl.when(c >= P_SLOTS)
        def _():
            for kind in range(3):
                for cp in s_copies(c - P_SLOTS, kind):
                    cp.wait_send()

        @pl.when(c < 6)
        def _():
            wslot = lax.rem(c // 2, 2)

            @pl.when(lax.rem(c, 2) == 0)
            def _():
                w_wait(wslot)

            rows = pl.ds(pl.multiple_of(lax.rem(c, 2) * 512, 512), 512)

            @pl.loop(0, 8)
            def _(q):
                o = jnp.dot(heads[rows, :], w[wslot, q], preferred_element_type=F32).astype(BF16)
                p[slot, q // 2, lax.rem(q, 2) * 2] = o[:, :128]
                p[slot, q // 2, lax.rem(q, 2) * 2 + 1] = o[:, 128:]

            @pl.when(c == 1)
            def _():
                w_start(2, 0)

            @pl.when(c == 3)
            def _():
                w_start_tail(1)

        @pl.when(c == 6)
        def _():
            tail = w.at[1, :, :, pl.ds(0, 128)]
            pltpu.make_async_copy(tail, tail, w_sem.at[1]).wait()
            lane = lax.broadcasted_iota(jnp.int32, (512, 128), 1)

            @pl.loop(0, 8)
            def _(q):
                wq = w[1, q, :, pl.ds(0, 128)]
                top = jnp.dot(heads[pl.ds(0, 512), :], wq, preferred_element_type=F32)
                bottom = jnp.dot(heads[pl.ds(512, 512), :], wq, preferred_element_type=F32)
                p[slot, q // 2, lax.rem(q, 2) * 2] = jnp.where(lane < 64, top, roll64(bottom)).astype(BF16)
                p[slot, q // 2, lax.rem(q, 2) * 2 + 1] = jnp.where(lane < 64, roll64(top), bottom).astype(BF16)

        start(s_copies(c, 0))
        start(s_copies(c, 1))

    def pass_on(c):
        slot, n1 = lax.rem(c, P_SLOTS), lax.rem(c, S1_SLOTS)
        got(s_copies(c, 0))
        for dim in range(2):
            for way in range(2):
                dest = off(coord[dim], 1 if way == 0 else 3)
                ref = piece(slot, dim, dest, way)
                ref[...] = (ref[...].astype(F32) + s1r[n1, dim, way].astype(F32)).astype(BF16)
        start(s_copies(c, 2))

    def reduce_first(c):
        slot, n5, rs = lax.rem(c, P_SLOTS), lax.rem(c, S23_SLOTS), lax.rem(c, R_SLOTS)
        got(s_copies(c, 1))
        got(s_copies(c, 2))
        for dim in range(2):
            for half in range(2):
                mine = piece(slot, dim, coord[dim], half)[...].astype(F32)
                total = mine + s3r[n5, dim, half].astype(F32) + s2r[n5, dim, 1 - half].astype(F32)
                r[rs, dim, :, pl.ds(half * 128, 128), :] = total.astype(BF16)
        start(t_copies(c, 0))
        start(t_copies(c, 1))

    def pass_on_second(c):
        rs = lax.rem(c, R_SLOTS)
        got(t_copies(c, 0))
        for dim in range(2):
            for way in range(2):
                dest = off(coord[1 - dim], 1 if way == 0 else 3)
                ref = r.at[rs, dim, dest, pl.ds(way * 128, 128), :]
                ref[...] = (ref[...].astype(F32) + t1r[c, dim, way].astype(F32)).astype(BF16)
        start(t_copies(c, 2))

    def reduce_second(c):
        rs = lax.rem(c, R_SLOTS)
        got(t_copies(c, 1))
        got(t_copies(c, 2))
        for dim in range(2):
            for half in range(2):
                mine = r[rs, dim, coord[1 - dim], pl.ds(half * 128, 128), :].astype(F32)
                f[c, pl.ds(dim * 256 + half * 128, 128), :] = (
                    mine + t3r[c, dim, half].astype(F32) + t2r[c, dim, 1 - half].astype(F32))
        for kind in range(3):
            for cp in t_copies(c, kind):
                cp.wait_send()

    def l_copies(phase):
        copies = []
        for dim in range(2):
            me, to = coord[dim], ring[dim]
            other, to_other = coord[1 - dim], ring[1 - dim]
            mine = dim * 4 + me
            part = pl.ds(pl.multiple_of(other * 64, 64), 64)
            for k in range(1, 4):
                if phase == 0:
                    src, dst, dev = low.at[dim * 4 + off(me, k)], l1r.at[dim, k - 1], to[k]
                elif phase == 1:
                    src = mid.at[dim, pl.ds(pl.multiple_of(off(other, k) * 64, 64), 64), :]
                    dst, dev = l2r.at[dim, k - 1], to_other[k]
                elif phase == 2:
                    src = dst = lowf.at[mine, part, :]
                    dev = to_other[k]
                else:
                    src = dst = lowf.at[mine]
                    dev = to[k]
                copies.append(remote(src, dst, l_send.at[phase, dim, k - 1], l_recv.at[phase, dim, k - 1], dev))
        return copies

    def low_images():
        own_dn.wait()
        got(dn1[4:])
        got(dn2[2:])
        got(dn3)

        @pl.loop(0, 8)
        def _(q):
            rows = pl.ds(pl.multiple_of((q // 2) * 256, 256), 256)
            chosen = gdn[ids[q // 2, lax.rem(q, 2)]]
            low[q] = lax.dot_general(
                heads[rows, :], chosen, (((1,), (1,)), ((), ())), preferred_element_type=F32).astype(BF16)

        start(l_copies(0))

    def low_second():
        got(l_copies(0))
        for dim in range(2):
            total = low[dim * 4 + coord[dim]].astype(F32)
            for k in range(3):
                total = total + l1r[dim, k].astype(F32)
            mid[dim] = total.astype(BF16)
        start(l_copies(1))

    def low_third():
        got(l_copies(1))
        for dim in range(2):
            part = pl.ds(pl.multiple_of(coord[1 - dim] * 64, 64), 64)
            total = mid[dim, part, :].astype(F32)
            for k in range(3):
                total = total + l2r[dim, k].astype(F32)
            lowf[dim * 4 + coord[dim], part, :] = total.astype(BF16)
        start(l_copies(2))

    def low_fourth():
        got(l_copies(2))
        start(l_copies(3))

    @pl.loop(0, CHUNKS + LAG)
    def _(i):
        @pl.when(i < CHUNKS)
        def _():
            produce(i)

        @pl.when((i >= 1) & (i < CHUNKS + 1))
        def _():
            pass_on(i - 1)

        @pl.when((i >= 2) & (i < CHUNKS + 2))
        def _():
            reduce_first(i - 2)

        @pl.when((i >= 3) & (i < CHUNKS + 3))
        def _():
            pass_on_second(i - 3)

        @pl.when(i >= 4)
        def _():
            reduce_second(i - 4)

        @pl.when(i == 4)
        def _():
            got(dn1[:4])
            start(dn2)

        @pl.when(i == 6)
        def _():
            got(dn2[:2])
            start(dn3)
            start(up1)

        @pl.when(i == 7)
        def _():
            low_images()

        @pl.when(i == 8)
        def _():
            low_second()

        @pl.when(i == 9)
        def _():
            low_third()
            got(up1[:4])
            start(up2)

        @pl.when(i == 10)
        def _():
            low_fourth()

    for c in range(CHUNKS - P_SLOTS, CHUNKS):
        for kind in range(3):
            for cp in s_copies(c, kind):
                cp.wait_send()
    got(l_copies(3))
    got(up2[:2])
    start(up3)
    own_up.wait()
    got(up1[4:])
    got(up2[2:])
    got(up3)

    lane = lax.broadcasted_iota(jnp.int32, (256, 128), 1)
    for b in range(4):
        half, at_row = b // 2, (b % 2) * 256
        rows = pl.ds(b * 256, 256)
        lifted = None
        for k in range(2):
            li = lax.dot_general(
                lowf[b * 2 + k], gup[ids[b, k]], (((1,), (1,)), ((), ())),
                preferred_element_type=F32).astype(BF16).astype(F32)
            weight = jnp.broadcast_to(mix[k:k + 1, b * 256:(b + 1) * 256], (128, 256)).T
            li = [li[:, :128] * weight, li[:, 128:256] * weight, li[:, 256:384] * weight, li[:, 384:] * weight[:, :64]]
            lifted = li if lifted is None else [u + v for u, v in zip(lifted, li)]
        main = [f[2 * t + half, pl.ds(at_row, 256), :] for t in range(3)]
        tail = f[6, pl.ds(at_row, 256), :]
        if half == 1:
            tail = roll64(tail)

        def write(tiles):
            for t in range(3):
                out[rows, pl.ds(t * 128, 128)] = (tiles[t] + lifted[t]).astype(BF16)
            out[rows, pl.ds(384, 64)] = (tiles[3][:, :64] + lifted[3]).astype(BF16)

        @pl.when(lax.rem(z, 2) == 0)
        def _():
            write(main + [tail])

        @pl.when(lax.rem(z, 2) == 1)
        def _():
            turned = [roll64(m) for m in main]
            write([
                jnp.where(lane < 64, tail, turned[0]),
                jnp.where(lane < 64, turned[0], turned[1]),
                jnp.where(lane < 64, turned[1], turned[2]),
                turned[2],
            ])

    for copies in (dn1, dn2, dn3, up1, up2, up3, l_copies(0), l_copies(1), l_copies(2), l_copies(3)):
        for cp in copies:
            cp.wait_send()


def local(latent, value_up, out_proj, adapter_down, adapter_up, pair_ids, mix_weights):
    rows = latent.shape[0]
    any_ = pl.BlockSpec(memory_space=pl.ANY)
    vmem = pl.BlockSpec(memory_space=pltpu.VMEM)
    smem = pl.BlockSpec(memory_space=pltpu.SMEM)
    dma = pltpu.SemaphoreType.DMA
    scratch = [
        pltpu.VMEM((4, 2048, 128), F32),
        pltpu.VMEM((8, 512, 128), BF16),
        pltpu.VMEM((rows, 1024), BF16),
        pltpu.VMEM((2, 8, 1024, 256), BF16),
        pltpu.VMEM((P_SLOTS, 4, 4, 512, 128), BF16),
        pltpu.VMEM((S1_SLOTS, 2, 2, 4, 128, 128), BF16),
        pltpu.VMEM((S23_SLOTS, 2, 2, 4, 128, 128), BF16),
        pltpu.VMEM((S23_SLOTS, 2, 2, 4, 128, 128), BF16),
        pltpu.VMEM((R_SLOTS, 2, 4, 256, 128), BF16),
        pltpu.VMEM((CHUNKS, 2, 2, 128, 128), BF16),
        pltpu.VMEM((CHUNKS, 2, 2, 128, 128), BF16),
        pltpu.VMEM((CHUNKS, 2, 2, 128, 128), BF16),
        pltpu.VMEM((CHUNKS, 512, 128), F32),
        pltpu.VMEM((32, 256, 1024), BF16),
        pltpu.VMEM((32, 448, 256), BF16),
        pltpu.VMEM((8, 256, 256), BF16),
        pltpu.VMEM((2, 3, 256, 256), BF16),
        pltpu.VMEM((2, 256, 256), BF16),
        pltpu.VMEM((2, 3, 64, 256), BF16),
        pltpu.VMEM((8, 256, 256), BF16),
        dma((2,)), dma, dma((2,)), dma((2,)),
        dma((3, CHUNKS, 2, 2)), dma((3, CHUNKS, 2, 2)),
        dma((3, CHUNKS, 2, 2)), dma((3, CHUNKS, 2, 2)),
        dma((32,)), dma((32,)),
        dma((4, 2, 3)), dma((4, 2, 3)),
    ]
    return pl.pallas_call(
        kernel,
        out_shape=jax.ShapeDtypeStruct((rows, adapter_up.shape[2]), BF16),
        in_specs=[any_, any_, any_, any_, any_, smem, vmem],
        out_specs=vmem,
        scratch_shapes=scratch,
        compiler_params=pltpu.CompilerParams(
            collective_id=1, has_side_effects=True, vmem_limit_bytes=64 << 20),
        name="project",
    )(
        latent.reshape(rows * 8, 512), value_up, out_proj, adapter_down,
        jnp.swapaxes(adapter_up, 1, 2), pair_ids, mix_weights,
    )


def solution(mesh):
    placed = (
        P("grp", "dev", None),
        P("dev", None, None),
        P("dev", None),
        P("grp", None, "dev"),
        P("grp", None, "dev"),
        P("grp", None),
        P(None, "grp"),
    )
    return jax.shard_map(
        local, mesh=mesh, in_specs=placed, out_specs=P("grp", "dev"), check_vma=False
    )
```

```python
import functools

import jax
import jax.numpy as jnp
from jax import lax
from jax.experimental import pallas as pl
from jax.experimental.pallas import tpu as pltpu
from jax.sharding import PartitionSpec as P

MESH = pl.DeviceIdType.MESH
F32 = jnp.float32
BF16 = jnp.bfloat16
CHUNKS = 7
LAG = 4
P_SLOTS = 3
S1_SLOTS = 3
S23_SLOTS = 5
R_SLOTS = 3


def roll64(x):
    return pltpu.roll(x, 64, 1)


def kernel(
    latent, value_up, out_proj, down, up_t, ids, mix, out,
    wide, vup, heads, w, p, s1r, s23r, r, t1r, t23r, f,
    gdn, gup, low, l1r, mid, l2r, lowf, staged,
    lat_sem, vup_sem, w_sem, own_sem, out_sem,
    s_send, s1_recv, s23_recv, t_send, t1_recv, t23_recv, y_send, y_recv, l_send, l_recv,
):
    g = lax.axis_index("grp")
    d = lax.axis_index("dev")
    y, core = g // 2, g % 2
    x, z = d // 4, d % 4

    def at(yy=None, cc=None, xx=None, zz=None):
        yy = y if yy is None else yy
        cc = core if cc is None else cc
        xx = x if xx is None else xx
        zz = z if zz is None else zz
        return (yy * 2 + cc, xx * 4 + zz)

    def off(v, k):
        return lax.rem(v + k, 4)

    y_up, y_down, sibling = at(yy=off(y, 1)), at(yy=off(y, 3)), at(cc=1 - core)
    x_at = [None] + [at(xx=off(x, k)) for k in (1, 2, 3)]
    z_at = [None] + [at(zz=off(z, k)) for k in (1, 2, 3)]

    def arrived(ref, sem):
        pltpu.make_async_copy(ref, ref, sem).wait()

    def remote(src, dst, send, recv, to):
        return pltpu.make_async_remote_copy(
            src_ref=src, dst_ref=dst, send_sem=send, recv_sem=recv, device_id=to, device_id_type=MESH
        )

    barrier = pltpu.get_barrier_semaphore()
    for n in x_at[1:] + z_at[1:] + [y_up, y_down, sibling]:
        pl.semaphore_signal(barrier, inc=1, device_id=n, device_id_type=MESH)

    def lat_start(c, slot):
        for k in range(4):
            for m in range(4):
                pltpu.make_async_copy(
                    latent.at[pl.ds(pl.multiple_of(c * 2048 + m * 512, 512), 512), pl.ds(k * 128, 128)],
                    p.at[slot + 1, k, m], lat_sem.at[slot]).start()

    def lat_wait(slot):
        arrived(p.at[slot + 1], lat_sem.at[slot])

    def w_start(t, slot):
        @pl.loop(0, 8)
        def _(q):
            for par in range(2):
                pltpu.make_async_copy(
                    out_proj.at[:, pl.ds(pl.multiple_of(q * 896 + par * 512 + t * 128, 128), 128)],
                    w.at[slot, q, :, pl.ds(par * 128, 128)], w_sem.at[slot]).start()

    def w_start_tail(slot):
        @pl.loop(0, 8)
        def _(q):
            pltpu.make_async_copy(
                out_proj.at[:, pl.ds(pl.multiple_of(q * 896 + 384, 128), 128)],
                w.at[slot, q, :, pl.ds(0, 128)], w_sem.at[slot]).start()

    def w_wait(slot):
        arrived(w.at[slot], w_sem.at[slot])

    vup_copy = pltpu.make_async_copy(value_up, vup, vup_sem)
    vup_copy.start()
    lat_start(0, 0)
    lat_start(1, 1)
    w_start(0, 0)
    pl.semaphore_wait(barrier, 9)

    own = g * 4

    def block(yy, cc):
        return (yy * 2 + cc) * 4

    below, above, across = block(off(y, 3), core), block(off(y, 1), core), block(off(y, 2), core)

    class Gather:
        def __init__(self, kind, src, gathered):
            self.kind, self.src, self.all = kind, src, gathered

        def send(self, source, unit, count, sem, to):
            remote(source, self.all.at[pl.ds(unit, count)], y_send.at[self.kind], y_recv.at[self.kind, sem], to).start()

        def own(self, k):
            self.send(self.src.at[pl.ds(k, 1)], own + k, 1, min(k, 2), y_up)
            m = (k + 2) % 4
            self.send(self.src.at[pl.ds(m, 1)], own + m, 1, 4 + min(k, 2), y_down)

        def pass_on(self, k):
            self.wait(k, 1)
            self.send(self.all.at[pl.ds(below + k, 1)], below + k, 1, 3, y_up)
            self.wait(4 + k, 1)
            self.send(self.all.at[pl.ds(above + 2 + k, 1)], above + 2 + k, 1, 7, y_down)

        def share_own(self):
            self.send(self.src, own, 4, 8, sibling)

        def share_near(self):
            self.wait(2, 2)
            self.wait(6, 2)
            self.send(self.all.at[pl.ds(below, 4)], below, 4, 9, sibling)
            self.send(self.all.at[pl.ds(above, 4)], above, 4, 9, sibling)

        def share_far(self):
            self.wait(3, 2)
            self.wait(7, 2)
            self.send(self.all.at[pl.ds(across, 4)], across, 4, 10, sibling)

        def wait(self, sem, units):
            arrived(self.all.at[pl.ds(0, units)], y_recv.at[self.kind, sem])

        def wait_shared(self):
            self.wait(8, 4)
            self.wait(9, 8)
            self.wait(10, 4)

        def wait_sent(self):
            arrived(self.all.at[pl.ds(0, 28)], y_send.at[self.kind])

    dn = Gather(0, down, gdn)
    up = Gather(1, up_t, gup)

    def start(copies):
        for c in copies:
            c.start()

    dn.own(0)
    dn.own(1)
    own_dn = pltpu.make_async_copy(down, gdn.at[pl.ds(own, 4)], own_sem.at[0])
    own_up = pltpu.make_async_copy(up_t, gup.at[pl.ds(own, 4)], own_sem.at[1])

    vup_copy.wait()

    def heads_rows(c):
        slot = c % 2
        lat_wait(slot)
        for k in range(4):
            for m in range(4):
                wide[k, pl.ds(m * 512, 512), :] = p[slot + 1, k, m].astype(F32)

        if c < 2:
            lat_start(c + 2, slot)
        for h in range(8):
            xh = jnp.concatenate([wide[k, pl.ds(h, 256, stride=8), :] for k in range(4)], axis=1).astype(BF16)
            heads[pl.ds(c * 256, 256), pl.ds(h * 128, 128)] = jnp.dot(
                xh, vup[h], preferred_element_type=F32).astype(BF16)

    heads_rows(0)
    heads_rows(1)
    w_start(1, 1)

    coord = (x, z)
    ring = (x_at, z_at)

    def piece(slot, dim, dest, half):
        rows = pl.ds(dim * 256 + half * 128, 128)
        return p.at[slot, dest, :, rows, :] if dim == 0 else p.at[slot, :, dest, rows, :]

    def s_copies(c, kind):
        slot, n1, n5 = lax.rem(c, P_SLOTS), lax.rem(c, S1_SLOTS), lax.rem(c, S23_SLOTS)
        copies = []
        for dim in range(2):
            me, to = coord[dim], ring[dim]
            plus, opp, minus = off(me, 1), off(me, 2), off(me, 3)
            what = {0: ((opp, 0), (opp, 1)), 1: ((plus, 1), (minus, 0)), 2: ((plus, 0), (minus, 1))}[kind]
            land = (s1r.at[n1], s23r.at[n5, 0], s23r.at[n5, 1])[kind]
            sem = s1_recv.at[n1] if kind == 0 else s23_recv.at[n5]
            for way in range(2):
                dest, half = what[way]
                copies.append(remote(
                    piece(slot, dim, dest, half), land.at[dim, way],
                    s_send.at[slot], sem, to[1] if way == 0 else to[3]))
        return copies

    def t_copies(c, kind):
        slot, n3, n5 = lax.rem(c, R_SLOTS), lax.rem(c, S1_SLOTS), lax.rem(c, S23_SLOTS)
        copies = []
        for dim in range(2):
            me, to = coord[1 - dim], ring[1 - dim]
            plus, opp, minus = off(me, 1), off(me, 2), off(me, 3)
            what = {0: ((opp, 0), (opp, 1)), 1: ((plus, 1), (minus, 0)), 2: ((plus, 0), (minus, 1))}[kind]
            land = (t1r.at[n3], t23r.at[n5, 0], t23r.at[n5, 1])[kind]
            sem = t1_recv.at[n3] if kind == 0 else t23_recv.at[n5]
            for way in range(2):
                dest, half = what[way]
                copies.append(remote(
                    r.at[slot, dim, dest, pl.ds(half * 128, 128), :], land.at[dim, way],
                    t_send.at[slot], sem, to[1] if way == 0 else to[3]))
        return copies

    def s_sent(slot):
        arrived(p.at[slot, pl.ds(0, 3)], s_send.at[slot])

    def produce(c):
        slot = lax.rem(c, P_SLOTS)

        @pl.when(c >= P_SLOTS)
        def _():
            s_sent(slot)

        @pl.when(c < 6)
        def _():
            wslot = lax.rem(c // 2, 2)

            @pl.when(lax.rem(c, 2) == 0)
            def _():
                w_wait(wslot)

            rows = pl.ds(pl.multiple_of(lax.rem(c, 2) * 512, 512), 512)

            @pl.loop(0, 8)
            def _(q):
                o = jnp.dot(heads[rows, :], w[wslot, q], preferred_element_type=F32).astype(BF16)
                p[slot, q // 2, lax.rem(q, 2) * 2] = o[:, :128]
                p[slot, q // 2, lax.rem(q, 2) * 2 + 1] = o[:, 128:]

            @pl.when(c == 1)
            def _():
                w_start(2, 0)

            @pl.when(c == 3)
            def _():
                w_start_tail(1)

        @pl.when(c == 6)
        def _():
            arrived(w.at[1, :, :, pl.ds(0, 128)], w_sem.at[1])
            lane = lax.broadcasted_iota(jnp.int32, (512, 128), 1)

            @pl.loop(0, 8)
            def _(q):
                wq = w[1, q, :, pl.ds(0, 128)]
                top = jnp.dot(heads[pl.ds(0, 512), :], wq, preferred_element_type=F32)
                bottom = jnp.dot(heads[pl.ds(512, 512), :], wq, preferred_element_type=F32)
                p[slot, q // 2, lax.rem(q, 2) * 2] = jnp.where(lane < 64, top, roll64(bottom)).astype(BF16)
                p[slot, q // 2, lax.rem(q, 2) * 2 + 1] = jnp.where(lane < 64, roll64(top), bottom).astype(BF16)

        start(s_copies(c, 0))
        start(s_copies(c, 1))

    def pass_on(c):
        slot, n1 = lax.rem(c, P_SLOTS), lax.rem(c, S1_SLOTS)
        arrived(s1r.at[n1], s1_recv.at[n1])
        for dim in range(2):
            for way in range(2):
                dest = off(coord[dim], 1 if way == 0 else 3)
                ref = piece(slot, dim, dest, way)
                ref[...] = (ref[...].astype(F32) + s1r[n1, dim, way].astype(F32)).astype(BF16)
        start(s_copies(c, 2))

    def reduce_first(c):
        slot, n5, rs = lax.rem(c, P_SLOTS), lax.rem(c, S23_SLOTS), lax.rem(c, R_SLOTS)
        arrived(s23r.at[n5], s23_recv.at[n5])
        for dim in range(2):
            for half in range(2):
                mine = piece(slot, dim, coord[dim], half)[...].astype(F32)
                total = mine + s23r[n5, 1, dim, half].astype(F32) + s23r[n5, 0, dim, 1 - half].astype(F32)
                r[rs, dim, :, pl.ds(half * 128, 128), :] = total.astype(BF16)
        start(t_copies(c, 0))
        start(t_copies(c, 1))

    def pass_on_second(c):
        rs, n3 = lax.rem(c, R_SLOTS), lax.rem(c, S1_SLOTS)
        arrived(t1r.at[n3], t1_recv.at[n3])
        for dim in range(2):
            for way in range(2):
                dest = off(coord[1 - dim], 1 if way == 0 else 3)
                ref = r.at[rs, dim, dest, pl.ds(way * 128, 128), :]
                ref[...] = (ref[...].astype(F32) + t1r[n3, dim, way].astype(F32)).astype(BF16)
        start(t_copies(c, 2))

    def reduce_second(c):
        rs, n5 = lax.rem(c, R_SLOTS), lax.rem(c, S23_SLOTS)
        arrived(t23r.at[n5], t23_recv.at[n5])
        for dim in range(2):
            for half in range(2):
                mine = r[rs, dim, coord[1 - dim], pl.ds(half * 128, 128), :].astype(F32)
                f[c, pl.ds(dim * 256 + half * 128, 128), :] = (
                    mine + t23r[n5, 1, dim, half].astype(F32) + t23r[n5, 0, dim, 1 - half].astype(F32))
        arrived(r.at[rs, :, pl.ds(0, 3)], t_send.at[rs])

    def l_copies(phase):
        copies = []
        for dim in range(2):
            me, to = coord[dim], ring[dim]
            other, to_other = coord[1 - dim], ring[1 - dim]
            mine = dim * 4 + me
            part = pl.ds(pl.multiple_of(other * 64, 64), 64)
            for k in range(1, 4):
                if phase == 0:
                    src, dst, dev = low.at[dim * 4 + off(me, k)], l1r.at[dim, k - 1], to[k]
                elif phase == 1:
                    src = mid.at[dim, pl.ds(pl.multiple_of(off(other, k) * 64, 64), 64), :]
                    dst, dev = l2r.at[dim, k - 1], to_other[k]
                elif phase == 2:
                    src = dst = lowf.at[mine, part, :]
                    dev = to_other[k]
                else:
                    src = dst = lowf.at[mine]
                    dev = to[k]
                copies.append(remote(src, dst, l_send.at[phase], l_recv.at[phase], dev))
        return copies

    def low_images():
        own_dn.wait()
        dn.wait_shared()

        @pl.loop(0, 8)
        def _(q):
            rows = pl.ds(pl.multiple_of((q // 2) * 256, 256), 256)
            chosen = gdn[ids[lax.rem(q, 2), q // 2]]
            low[q] = lax.dot_general(
                heads[rows, :], chosen, (((1,), (1,)), ((), ())), preferred_element_type=F32).astype(BF16)

        start(l_copies(0))

    def low_second():
        arrived(l1r, l_recv.at[0])
        for dim in range(2):
            total = low[dim * 4 + coord[dim]].astype(F32)
            for k in range(3):
                total = total + l1r[dim, k].astype(F32)
            mid[dim] = total.astype(BF16)
        start(l_copies(1))

    def low_third():
        arrived(l2r, l_recv.at[1])
        for dim in range(2):
            part = pl.ds(pl.multiple_of(coord[1 - dim] * 64, 64), 64)
            total = mid[dim, part, :].astype(F32)
            for k in range(3):
                total = total + l2r[dim, k].astype(F32)
            lowf[dim * 4 + coord[dim], part, :] = total.astype(BF16)
        start(l_copies(2))

    def low_fourth():
        arrived(l2r, l_recv.at[2])
        start(l_copies(3))

    @pl.loop(0, CHUNKS + LAG)
    def _(i):
        @pl.when(i < CHUNKS)
        def _():
            produce(i)

        @pl.when((i >= 1) & (i < CHUNKS + 1))
        def _():
            pass_on(i - 1)

        @pl.when((i >= 2) & (i < CHUNKS + 2))
        def _():
            reduce_first(i - 2)

        @pl.when((i >= 3) & (i < CHUNKS + 3))
        def _():
            pass_on_second(i - 3)

        @pl.when(i >= 4)
        def _():
            reduce_second(i - 4)

        @pl.when(i == 0)
        def _():
            dn.own(2)
            own_dn.start()
            heads_rows(2)
            heads_rows(3)
            dn.share_own()

        @pl.when(i == 1)
        def _():
            dn.own(3)
            own_up.start()

        @pl.when(i == 3)
        def _():
            dn.pass_on(0)

        @pl.when(i == 4)
        def _():
            dn.pass_on(1)

        @pl.when(i == 5)
        def _():
            dn.share_near()

        @pl.when(i == 6)
        def _():
            up.own(0)
            up.own(1)
            dn.share_far()
            up.own(2)
            up.own(3)
            up.share_own()

        @pl.when(i == 7)
        def _():
            low_images()

        @pl.when(i == 8)
        def _():
            low_second()

        @pl.when(i == 9)
        def _():
            low_third()
            up.pass_on(0)
            up.pass_on(1)

        @pl.when(i == 10)
        def _():
            low_fourth()

    for c in range(CHUNKS - P_SLOTS, CHUNKS):
        s_sent(c % P_SLOTS)
    up.share_near()
    arrived(lowf.at[pl.ds(0, 6)], l_recv.at[3])
    up.share_far()
    own_up.wait()
    up.wait_shared()

    lane = lax.broadcasted_iota(jnp.int32, (256, 128), 1)
    for b in range(4):
        half, at_row = b // 2, (b % 2) * 256
        rows = pl.ds(b * 256, 256)
        lifted = None
        for k in range(2):
            li = lax.dot_general(
                lowf[b * 2 + k], gup[ids[k, b]], (((1,), (1,)), ((), ())),
                preferred_element_type=F32).astype(BF16).astype(F32)
            weight = jnp.broadcast_to(mix[k:k + 1, b * 256:(b + 1) * 256], (128, 256)).T
            li = [li[:, :128] * weight, li[:, 128:256] * weight, li[:, 256:384] * weight, li[:, 384:] * weight[:, :64]]
            lifted = li if lifted is None else [u + v for u, v in zip(lifted, li)]
        main = [f[2 * t + half, pl.ds(at_row, 256), :] for t in range(3)]
        tail = f[6, pl.ds(at_row, 256), :]
        if half == 1:
            tail = roll64(tail)

        def write(tiles):
            for t in range(3):
                staged[rows, pl.ds(t * 128, 128)] = (tiles[t] + lifted[t]).astype(BF16)
            staged[rows, pl.ds(384, 64)] = (tiles[3][:, :64] + lifted[3]).astype(BF16)

        @pl.when(lax.rem(z, 2) == 0)
        def _():
            write(main + [tail])

        @pl.when(lax.rem(z, 2) == 1)
        def _():
            turned = [roll64(m) for m in main]
            write([
                jnp.where(lane < 64, tail, turned[0]),
                jnp.where(lane < 64, turned[0], turned[1]),
                jnp.where(lane < 64, turned[1], turned[2]),
                turned[2],
            ])

        pltpu.make_async_copy(staged.at[rows], out.at[rows], out_sem).start()

    arrived(staged, out_sem)
    dn.wait_sent()
    up.wait_sent()
    for phase, ref in enumerate((low.at[pl.ds(0, 6)], l2r, l2r, low.at[pl.ds(0, 6)])):
        arrived(ref, l_send.at[phase])


def local(latent, value_up, out_proj, adapter_down, adapter_up, pair_ids, mix_weights):
    rows = latent.shape[0]
    any_ = pl.BlockSpec(memory_space=pl.ANY)
    vmem = pl.BlockSpec(memory_space=pltpu.VMEM)
    smem = pl.BlockSpec(memory_space=pltpu.SMEM)
    dma = pltpu.SemaphoreType.DMA
    scratch = [
        pltpu.VMEM((4, 2048, 128), F32),
        pltpu.VMEM((8, 512, 128), BF16),
        pltpu.VMEM((rows, 1024), BF16),
        pltpu.VMEM((2, 8, 1024, 256), BF16),
        pltpu.VMEM((P_SLOTS, 4, 4, 512, 128), BF16),
        pltpu.VMEM((S1_SLOTS, 2, 2, 4, 128, 128), BF16),
        pltpu.VMEM((S23_SLOTS, 2, 2, 2, 4, 128, 128), BF16),
        pltpu.VMEM((R_SLOTS, 2, 4, 256, 128), BF16),
        pltpu.VMEM((S1_SLOTS, 2, 2, 128, 128), BF16),
        pltpu.VMEM((S23_SLOTS, 2, 2, 2, 128, 128), BF16),
        pltpu.VMEM((CHUNKS, 512, 128), F32),
        pltpu.VMEM((32, 256, 1024), BF16),
        pltpu.VMEM((32, 448, 256), BF16),
        pltpu.VMEM((8, 256, 256), BF16),
        pltpu.VMEM((2, 3, 256, 256), BF16),
        pltpu.VMEM((2, 256, 256), BF16),
        pltpu.VMEM((2, 3, 64, 256), BF16),
        pltpu.VMEM((8, 256, 256), BF16),
        pltpu.VMEM((rows, 448), BF16),
        dma((2,)), dma, dma((2,)), dma((2,)), dma,
        dma((P_SLOTS,)), dma((S1_SLOTS,)), dma((S23_SLOTS,)),
        dma((R_SLOTS,)), dma((S1_SLOTS,)), dma((S23_SLOTS,)),
        dma((2,)), dma((2, 11)), dma((4,)), dma((4,)),
    ]
    return pl.pallas_call(
        kernel,
        out_shape=jax.ShapeDtypeStruct((rows, adapter_up.shape[2]), BF16),
        in_specs=[any_, any_, any_, any_, any_, smem, vmem],
        out_specs=any_,
        scratch_shapes=scratch,
        compiler_params=pltpu.CompilerParams(
            collective_id=1, has_side_effects=True, vmem_limit_bytes=64 << 20),
        name="project",
    )(
        latent.reshape(rows * 8, 512), value_up, out_proj, adapter_down,
        jnp.swapaxes(adapter_up, 1, 2), pair_ids.T, mix_weights,
    )


def solution(mesh):
    placed = (
        P("grp", "dev", None),
        P("dev", None, None),
        P("dev", None),
        P("grp", None, "dev"),
        P("grp", None, "dev"),
        P("grp", None),
        P(None, "grp"),
    )
    return jax.shard_map(
        local, mesh=mesh, in_specs=placed, out_specs=P("grp", "dev"), check_vma=False
    )
```

```python
import functools

import jax
import jax.numpy as jnp
from jax import lax
from jax.experimental import pallas as pl
from jax.experimental.pallas import tpu as pltpu
from jax.sharding import PartitionSpec as P

MESH = pl.DeviceIdType.MESH
F32 = jnp.float32
BF16 = jnp.bfloat16
CHUNKS = 14
LAG = 2
P_SLOTS = 3
S1_SLOTS = 5
S23_SLOTS = 8
R_SLOTS = 5


def roll64(x):
    return pltpu.roll(x, 64, 1)


def kernel(
    latent, value_up, out_proj, down, up_t, ids, mix, out,
    lat, wide, vup, heads, w, p, s1r, s23r, r, t1r, t23r, f,
    gdn, gup, low, l1r, mid, l2r, lowf, staged,
    lat_sem, vup_sem, w_sem, own_sem, out_sem,
    s_send, s1_recv, s23_recv, t_send, t1_recv, t23_recv, y_send, y_recv, l_send, l_recv,
):
    g = lax.axis_index("grp")
    d = lax.axis_index("dev")
    y, core = g // 2, g % 2
    x, z = d // 4, d % 4

    def at(yy=None, cc=None, xx=None, zz=None):
        yy = y if yy is None else yy
        cc = core if cc is None else cc
        xx = x if xx is None else xx
        zz = z if zz is None else zz
        return (yy * 2 + cc, xx * 4 + zz)

    def off(v, k):
        return lax.rem(v + k, 4)

    y_up, y_down, sibling = at(yy=off(y, 1)), at(yy=off(y, 3)), at(cc=1 - core)
    x_at = [None] + [at(xx=off(x, k)) for k in (1, 2, 3)]
    z_at = [None] + [at(zz=off(z, k)) for k in (1, 2, 3)]

    def arrived(ref, sem):
        pltpu.make_async_copy(ref, ref, sem).wait()

    def remote(src, dst, send, recv, to):
        return pltpu.make_async_remote_copy(
            src_ref=src, dst_ref=dst, send_sem=send, recv_sem=recv, device_id=to, device_id_type=MESH
        )

    barrier = pltpu.get_barrier_semaphore()
    for n in x_at[1:] + z_at[1:] + [y_up, y_down, sibling]:
        pl.semaphore_signal(barrier, inc=1, device_id=n, device_id_type=MESH)

    def lat_start(c, slot):
        for k in range(4):
            pltpu.make_async_copy(
                latent.at[pl.ds(pl.multiple_of(c * 2048, 2048), 2048), pl.ds(k * 128, 128)],
                lat.at[slot, k], lat_sem.at[slot]).start()

    def w_start(t, slot):
        @pl.loop(0, 8)
        def _(q):
            for par in range(2):
                pltpu.make_async_copy(
                    out_proj.at[:, pl.ds(pl.multiple_of(q * 896 + par * 512 + t * 128, 128), 128)],
                    w.at[slot, q, :, pl.ds(par * 128, 128)], w_sem.at[slot]).start()

    def w_start_tail(slot):
        @pl.loop(0, 8)
        def _(q):
            pltpu.make_async_copy(
                out_proj.at[:, pl.ds(pl.multiple_of(q * 896 + 384, 128), 128)],
                w.at[slot, q, :, pl.ds(0, 128)], w_sem.at[slot]).start()

    def w_wait(slot):
        arrived(w.at[slot], w_sem.at[slot])

    vup_copy = pltpu.make_async_copy(value_up, vup, vup_sem)
    vup_copy.start()
    lat_start(0, 0)
    lat_start(1, 1)
    w_start(0, 0)
    pl.semaphore_wait(barrier, 9)

    own = g * 4

    def block(yy, cc):
        return (yy * 2 + cc) * 4

    below, above, across = block(off(y, 3), core), block(off(y, 1), core), block(off(y, 2), core)

    class Gather:
        def __init__(self, kind, src, gathered):
            self.kind, self.src, self.all = kind, src, gathered

        def send(self, source, unit, count, sem, to):
            remote(source, self.all.at[pl.ds(unit, count)], y_send.at[self.kind], y_recv.at[self.kind, sem], to).start()

        def own(self, k):
            self.send(self.src.at[pl.ds(k, 1)], own + k, 1, min(k, 2), y_up)
            m = (k + 2) % 4
            self.send(self.src.at[pl.ds(m, 1)], own + m, 1, 4 + min(k, 2), y_down)

        def pass_on(self, k):
            self.wait(k, 1)
            self.send(self.all.at[pl.ds(below + k, 1)], below + k, 1, 3, y_up)
            self.wait(4 + k, 1)
            self.send(self.all.at[pl.ds(above + 2 + k, 1)], above + 2 + k, 1, 7, y_down)

        def share_own(self):
            self.send(self.src, own, 4, 8, sibling)

        def share_near(self):
            self.wait(2, 2)
            self.wait(6, 2)
            self.send(self.all.at[pl.ds(below, 4)], below, 4, 9, sibling)
            self.send(self.all.at[pl.ds(above, 4)], above, 4, 9, sibling)

        def share_far(self):
            self.wait(3, 2)
            self.wait(7, 2)
            self.send(self.all.at[pl.ds(across, 4)], across, 4, 10, sibling)

        def wait(self, sem, units):
            arrived(self.all.at[pl.ds(0, units)], y_recv.at[self.kind, sem])

        def wait_shared(self):
            self.wait(8, 4)
            self.wait(9, 8)
            self.wait(10, 4)

        def wait_sent(self):
            arrived(self.all.at[pl.ds(0, 28)], y_send.at[self.kind])

    dn = Gather(0, down, gdn)
    up = Gather(1, up_t, gup)

    def start(copies):
        for c in copies:
            c.start()

    dn.own(0)
    dn.own(1)
    own_dn = pltpu.make_async_copy(down, gdn.at[pl.ds(own, 4)], own_sem.at[0])
    own_up = pltpu.make_async_copy(up_t, gup.at[pl.ds(own, 4)], own_sem.at[1])

    vup_copy.wait()

    def heads_rows(c):
        slot = lax.rem(c, 2)
        arrived(lat.at[slot], lat_sem.at[slot])
        for k in range(4):
            wide[k] = lat[slot, k].astype(F32)

        @pl.when(c < 2)
        def _():
            lat_start(c + 2, slot)

        for h in range(8):
            xh = jnp.concatenate([wide[k, pl.ds(h, 256, stride=8), :] for k in range(4)], axis=1).astype(BF16)
            heads[pl.ds(pl.multiple_of(c * 256, 256), 256), pl.ds(h * 128, 128)] = jnp.dot(
                xh, vup[h], preferred_element_type=F32).astype(BF16)

    heads_rows(jnp.int32(0))
    heads_rows(jnp.int32(1))
    w_start(1, 1)

    coord = (x, z)
    ring = (x_at, z_at)

    def piece(c, dim, dest, half):
        slot = lax.rem(c // 2, P_SLOTS)
        rows = pl.ds(pl.multiple_of(lax.rem(c, 2) * 256 + dim * 128 + half * 64, 64), 64)
        return p.at[slot, dest, :, rows, :] if dim == 0 else p.at[slot, :, dest, rows, :]

    def s_copies(c, kind):
        slot, n1, n5 = lax.rem(c // 2, P_SLOTS), lax.rem(c, S1_SLOTS), lax.rem(c, S23_SLOTS)
        copies = []
        for dim in range(2):
            me, to = coord[dim], ring[dim]
            plus, opp, minus = off(me, 1), off(me, 2), off(me, 3)
            what = {0: ((opp, 0), (opp, 1)), 1: ((plus, 1), (minus, 0)), 2: ((plus, 0), (minus, 1))}[kind]
            land = (s1r.at[n1], s23r.at[n5, 0], s23r.at[n5, 1])[kind]
            sem = s1_recv.at[n1] if kind == 0 else s23_recv.at[n5]
            for way in range(2):
                dest, half = what[way]
                copies.append(remote(
                    piece(c, dim, dest, half), land.at[dim, way],
                    s_send.at[slot], sem, to[1] if way == 0 else to[3]))
        return copies

    def t_copies(c, kind):
        slot, n3, n5 = lax.rem(c, R_SLOTS), lax.rem(c, S1_SLOTS), lax.rem(c, S23_SLOTS)
        copies = []
        for dim in range(2):
            me, to = coord[1 - dim], ring[1 - dim]
            plus, opp, minus = off(me, 1), off(me, 2), off(me, 3)
            what = {0: ((opp, 0), (opp, 1)), 1: ((plus, 1), (minus, 0)), 2: ((plus, 0), (minus, 1))}[kind]
            land = (t1r.at[n3], t23r.at[n5, 0], t23r.at[n5, 1])[kind]
            sem = t1_recv.at[n3] if kind == 0 else t23_recv.at[n5]
            for way in range(2):
                dest, half = what[way]
                copies.append(remote(
                    r.at[slot, dim, dest, pl.ds(half * 64, 64), :], land.at[dim, way],
                    t_send.at[slot], sem, to[1] if way == 0 else to[3]))
        return copies

    def s_sent(slot):
        arrived(p.at[slot, pl.ds(0, 3)], s_send.at[slot])

    def produce(c):
        slot = lax.rem(c, P_SLOTS)

        @pl.when(c >= P_SLOTS)
        def _():
            s_sent(slot)

        @pl.when(c < 6)
        def _():
            wslot = lax.rem(c // 2, 2)

            @pl.when(lax.rem(c, 2) == 0)
            def _():
                w_wait(wslot)

            rows = pl.ds(pl.multiple_of(lax.rem(c, 2) * 512, 512), 512)

            @pl.loop(0, 8)
            def _(q):
                o = jnp.dot(heads[rows, :], w[wslot, q], preferred_element_type=F32).astype(BF16)
                p[slot, q // 2, lax.rem(q, 2) * 2] = o[:, :128]
                p[slot, q // 2, lax.rem(q, 2) * 2 + 1] = o[:, 128:]

            @pl.when(c == 1)
            def _():
                w_start(2, 0)

            @pl.when(c == 3)
            def _():
                w_start_tail(1)

        @pl.when(c == 6)
        def _():
            arrived(w.at[1, :, :, pl.ds(0, 128)], w_sem.at[1])
            lane = lax.broadcasted_iota(jnp.int32, (512, 128), 1)

            @pl.loop(0, 8)
            def _(q):
                wq = w[1, q, :, pl.ds(0, 128)]
                top = jnp.dot(heads[pl.ds(0, 512), :], wq, preferred_element_type=F32)
                bottom = jnp.dot(heads[pl.ds(512, 512), :], wq, preferred_element_type=F32)
                p[slot, q // 2, lax.rem(q, 2) * 2] = jnp.where(lane < 64, top, roll64(bottom)).astype(BF16)
                p[slot, q // 2, lax.rem(q, 2) * 2 + 1] = jnp.where(lane < 64, roll64(top), bottom).astype(BF16)

    def pass_on(c):
        n1 = lax.rem(c, S1_SLOTS)
        arrived(s1r.at[n1], s1_recv.at[n1])
        for dim in range(2):
            for way in range(2):
                dest = off(coord[dim], 1 if way == 0 else 3)
                ref = piece(c, dim, dest, way)
                ref[...] = (ref[...].astype(F32) + s1r[n1, dim, way].astype(F32)).astype(BF16)
        start(s_copies(c, 2))

    def reduce_first(c):
        n5, rs = lax.rem(c, S23_SLOTS), lax.rem(c, R_SLOTS)
        arrived(s23r.at[n5], s23_recv.at[n5])
        for dim in range(2):
            for half in range(2):
                mine = piece(c, dim, coord[dim], half)[...].astype(F32)
                total = mine + s23r[n5, 1, dim, half].astype(F32) + s23r[n5, 0, dim, 1 - half].astype(F32)
                r[rs, dim, :, pl.ds(half * 64, 64), :] = total.astype(BF16)
        start(t_copies(c, 0))
        start(t_copies(c, 1))

    def pass_on_second(c):
        rs, n3 = lax.rem(c, R_SLOTS), lax.rem(c, S1_SLOTS)
        arrived(t1r.at[n3], t1_recv.at[n3])
        for dim in range(2):
            for way in range(2):
                dest = off(coord[1 - dim], 1 if way == 0 else 3)
                ref = r.at[rs, dim, dest, pl.ds(way * 64, 64), :]
                ref[...] = (ref[...].astype(F32) + t1r[n3, dim, way].astype(F32)).astype(BF16)
        start(t_copies(c, 2))

    def reduce_second(c):
        rs, n5 = lax.rem(c, R_SLOTS), lax.rem(c, S23_SLOTS)
        arrived(t23r.at[n5], t23_recv.at[n5])
        for dim in range(2):
            for half in range(2):
                mine = r[rs, dim, coord[1 - dim], pl.ds(half * 64, 64), :].astype(F32)
                f[c, pl.ds(dim * 128 + half * 64, 64), :] = (
                    mine + t23r[n5, 1, dim, half].astype(F32) + t23r[n5, 0, dim, 1 - half].astype(F32))
        arrived(r.at[rs, :, pl.ds(0, 3)], t_send.at[rs])

    def l_copies(phase):
        copies = []
        for dim in range(2):
            me, to = coord[dim], ring[dim]
            other, to_other = coord[1 - dim], ring[1 - dim]
            mine = dim * 4 + me
            part = pl.ds(pl.multiple_of(other * 64, 64), 64)
            for k in range(1, 4):
                if phase == 0:
                    src, dst, dev = low.at[dim * 4 + off(me, k)], l1r.at[dim, k - 1], to[k]
                elif phase == 1:
                    src = mid.at[dim, pl.ds(pl.multiple_of(off(other, k) * 64, 64), 64), :]
                    dst, dev = l2r.at[dim, k - 1], to_other[k]
                elif phase == 2:
                    src = dst = lowf.at[mine, part, :]
                    dev = to_other[k]
                else:
                    src = dst = lowf.at[mine]
                    dev = to[k]
                copies.append(remote(src, dst, l_send.at[phase], l_recv.at[phase], dev))
        return copies

    def low_images():
        own_dn.wait()
        dn.wait_shared()

        @pl.loop(0, 8)
        def _(q):
            rows = pl.ds(pl.multiple_of((q // 2) * 256, 256), 256)
            chosen = gdn[ids[lax.rem(q, 2), q // 2]]
            low[q] = lax.dot_general(
                heads[rows, :], chosen, (((1,), (1,)), ((), ())), preferred_element_type=F32).astype(BF16)

        start(l_copies(0))

    def low_second():
        arrived(l1r, l_recv.at[0])
        for dim in range(2):
            total = low[dim * 4 + coord[dim]].astype(F32)
            for k in range(3):
                total = total + l1r[dim, k].astype(F32)
            mid[dim] = total.astype(BF16)
        start(l_copies(1))

    def low_third():
        arrived(l2r, l_recv.at[1])
        for dim in range(2):
            part = pl.ds(pl.multiple_of(coord[1 - dim] * 64, 64), 64)
            total = mid[dim, part, :].astype(F32)
            for k in range(3):
                total = total + l2r[dim, k].astype(F32)
            lowf[dim * 4 + coord[dim], part, :] = total.astype(BF16)
        start(l_copies(2))

    def low_fourth():
        arrived(l2r, l_recv.at[2])
        start(l_copies(3))

    @pl.loop(0, CHUNKS + 4 * LAG)
    def _(i):
        @pl.when((i < CHUNKS) & (lax.rem(i, 2) == 0))
        def _():
            produce(i // 2)

        @pl.when(i < CHUNKS)
        def _():
            start(s_copies(i, 0))
            start(s_copies(i, 1))

        for stage, work in enumerate((pass_on, reduce_first, pass_on_second, reduce_second)):
            behind = (stage + 1) * LAG
            pl.when((i >= behind) & (i < CHUNKS + behind))(functools.partial(work, i - behind))

        @pl.when(i < 2)
        def _():
            heads_rows(i + 2)

        @pl.when(i == 0)
        def _():
            own_dn.start()

        @pl.when(i == 1)
        def _():
            dn.own(2)
            dn.share_own()
            own_up.start()

        @pl.when(i == 2)
        def _():
            dn.own(3)

        @pl.when(i == 5)
        def _():
            dn.pass_on(0)

        @pl.when(i == 7)
        def _():
            dn.pass_on(1)

        @pl.when(i == 9)
        def _():
            dn.share_near()

        @pl.when(i == 10)
        def _():
            up.own(0)
            up.own(1)

        @pl.when(i == 12)
        def _():
            dn.share_far()
            up.own(2)
            up.own(3)
            up.share_own()

        @pl.when(i == 13)
        def _():
            low_images()

        @pl.when(i == 15)
        def _():
            low_second()
            up.pass_on(0)

        @pl.when(i == 17)
        def _():
            low_third()
            up.pass_on(1)

        @pl.when(i == 19)
        def _():
            low_fourth()
            up.share_near()

    up.share_far()
    own_up.wait()

    lane = lax.broadcasted_iota(jnp.int32, (256, 128), 1)
    for b in range(4):
        main = [f[4 * t + b] for t in range(3)]
        tail = f[12 + b % 2]
        if b >= 2:
            tail = roll64(tail)

        def keep(tiles):
            for t in range(4):
                wide[b, pl.ds(t * 256, 256), :] = tiles[t]

        @pl.when(lax.rem(z, 2) == 0)
        def _():
            keep(main + [tail])

        @pl.when(lax.rem(z, 2) == 1)
        def _():
            turned = [roll64(m) for m in main]
            keep([
                jnp.where(lane < 64, tail, turned[0]),
                jnp.where(lane < 64, turned[0], turned[1]),
                jnp.where(lane < 64, turned[1], turned[2]),
                turned[2],
            ])

        for k in range(2):
            wide[b, pl.ds(1024 + k * 256, 256), :] = jnp.broadcast_to(mix[k:k + 1, b * 256:(b + 1) * 256], (128, 256)).T

    arrived(lowf.at[pl.ds(0, 6)], l_recv.at[3])
    up.wait_shared()

    for b in range(4):
        rows = pl.ds(b * 256, 256)
        first, second = [
            lax.dot_general(
                lowf[b * 2 + k], gup[ids[k, b]], (((1,), (1,)), ((), ())),
                preferred_element_type=F32).astype(BF16).astype(F32)
            for k in range(2)
        ]
        w0, w1 = wide[b, pl.ds(1024, 256), :], wide[b, pl.ds(1280, 256), :]
        for t in range(4):
            n = 128 if t < 3 else 64
            cols = slice(t * 128, t * 128 + n)
            mixed = wide[b, pl.ds(t * 256, 256), :][:, :n] + (w0[:, :n] * first[:, cols] + w1[:, :n] * second[:, cols])
            staged[rows, pl.ds(t * 128, n)] = mixed.astype(BF16)
        pltpu.make_async_copy(staged.at[rows], out.at[rows], out_sem).start()

    for slot in range(P_SLOTS):
        s_sent(slot)
    arrived(staged, out_sem)
    dn.wait_sent()
    up.wait_sent()
    for phase, ref in enumerate((low.at[pl.ds(0, 6)], l2r, l2r, low.at[pl.ds(0, 6)])):
        arrived(ref, l_send.at[phase])


def local(latent, value_up, out_proj, adapter_down, adapter_up, pair_ids, mix_weights):
    rows = latent.shape[0]
    any_ = pl.BlockSpec(memory_space=pl.ANY)
    vmem = pl.BlockSpec(memory_space=pltpu.VMEM)
    smem = pl.BlockSpec(memory_space=pltpu.SMEM)
    dma = pltpu.SemaphoreType.DMA
    scratch = [
        pltpu.VMEM((2, 4, 2048, 128), BF16),
        pltpu.VMEM((4, 2048, 128), F32),
        pltpu.VMEM((8, 512, 128), BF16),
        pltpu.VMEM((rows, 1024), BF16),
        pltpu.VMEM((2, 8, 1024, 256), BF16),
        pltpu.VMEM((P_SLOTS, 4, 4, 512, 128), BF16),
        pltpu.VMEM((S1_SLOTS, 2, 2, 4, 64, 128), BF16),
        pltpu.VMEM((S23_SLOTS, 2, 2, 2, 4, 64, 128), BF16),
        pltpu.VMEM((R_SLOTS, 2, 4, 128, 128), BF16),
        pltpu.VMEM((S1_SLOTS, 2, 2, 64, 128), BF16),
        pltpu.VMEM((S23_SLOTS, 2, 2, 2, 64, 128), BF16),
        pltpu.VMEM((CHUNKS, 256, 128), F32),
        pltpu.VMEM((32, 256, 1024), BF16),
        pltpu.VMEM((32, 448, 256), BF16),
        pltpu.VMEM((8, 256, 256), BF16),
        pltpu.VMEM((2, 3, 256, 256), BF16),
        pltpu.VMEM((2, 256, 256), BF16),
        pltpu.VMEM((2, 3, 64, 256), BF16),
        pltpu.VMEM((8, 256, 256), BF16),
        pltpu.VMEM((rows, 448), BF16),
        dma((2,)), dma, dma((2,)), dma((2,)), dma,
        dma((P_SLOTS,)), dma((S1_SLOTS,)), dma((S23_SLOTS,)),
        dma((R_SLOTS,)), dma((S1_SLOTS,)), dma((S23_SLOTS,)),
        dma((2,)), dma((2, 11)), dma((4,)), dma((4,)),
    ]
    return pl.pallas_call(
        kernel,
        out_shape=jax.ShapeDtypeStruct((rows, adapter_up.shape[2]), BF16),
        in_specs=[any_, any_, any_, any_, any_, smem, vmem],
        out_specs=any_,
        scratch_shapes=scratch,
        compiler_params=pltpu.CompilerParams(
            collective_id=1, has_side_effects=True, vmem_limit_bytes=64 << 20),
        name="project",
    )(
        latent.reshape(rows * 8, 512), value_up, out_proj, adapter_down,
        jnp.swapaxes(adapter_up, 1, 2), pair_ids.T, mix_weights,
    )


def solution(mesh):
    placed = (
        P("grp", "dev", None),
        P("dev", None, None),
        P("dev", None),
        P("grp", None, "dev"),
        P("grp", None, "dev"),
        P("grp", None),
        P(None, "grp"),
    )
    return jax.shard_map(
        local, mesh=mesh, in_specs=placed, out_specs=P("grp", "dev"), check_vma=False
    )
```

```python
import functools

import jax
import jax.numpy as jnp
from jax import lax
from jax.experimental import pallas as pl
from jax.experimental.pallas import tpu as pltpu
from jax.sharding import PartitionSpec as P

MESH = pl.DeviceIdType.MESH
F32 = jnp.float32
BF16 = jnp.bfloat16
CHUNKS = 14
LAG = 2
P_SLOTS = 3
S1_SLOTS = 5
S23_SLOTS = 8
R_SLOTS = 5


def roll64(x):
    return pltpu.roll(x, 64, 1)


def kernel(
    latent, value_up, out_proj, down, up_t, ids, mix, out,
    lat, wide, vup, heads, w, p, s1r, s23r, r, t1r, t23r, f,
    gdn, gup, low, l1r, mid, l2r, lowf, staged,
    lat_sem, vup_sem, w_sem, own_sem, out_sem,
    s_send, s1_recv, s23_recv, t_send, t1_recv, t23_recv, y_send, y_recv, l_send, l_recv,
):
    g = lax.axis_index("grp")
    d = lax.axis_index("dev")
    y, core = g // 2, g % 2
    x, z = d // 4, d % 4

    def at(yy=None, cc=None, xx=None, zz=None):
        yy = y if yy is None else yy
        cc = core if cc is None else cc
        xx = x if xx is None else xx
        zz = z if zz is None else zz
        return (yy * 2 + cc, xx * 4 + zz)

    def off(v, k):
        return lax.rem(v + k, 4)

    y_up, y_down, sibling = at(yy=off(y, 1)), at(yy=off(y, 3)), at(cc=1 - core)
    x_at = [None] + [at(xx=off(x, k)) for k in (1, 2, 3)]
    z_at = [None] + [at(zz=off(z, k)) for k in (1, 2, 3)]

    def arrived(ref, sem):
        pltpu.make_async_copy(ref, ref, sem).wait()

    def remote(src, dst, send, recv, to):
        return pltpu.make_async_remote_copy(
            src_ref=src, dst_ref=dst, send_sem=send, recv_sem=recv, device_id=to, device_id_type=MESH
        )

    barrier = pltpu.get_barrier_semaphore()
    for n in x_at[1:] + z_at[1:] + [y_up, y_down, sibling]:
        pl.semaphore_signal(barrier, inc=1, device_id=n, device_id_type=MESH)

    def lat_start(c, slot):
        for k in range(4):
            pltpu.make_async_copy(
                latent.at[pl.ds(pl.multiple_of(c * 2048, 2048), 2048), pl.ds(k * 128, 128)],
                lat.at[slot, k], lat_sem.at[slot]).start()

    def w_start(t, slot):
        @pl.loop(0, 8)
        def _(q):
            for par in range(2):
                pltpu.make_async_copy(
                    out_proj.at[:, pl.ds(pl.multiple_of(q * 896 + par * 512 + t * 128, 128), 128)],
                    w.at[slot, q, :, pl.ds(par * 128, 128)], w_sem.at[slot]).start()

    def w_start_tail(slot):
        @pl.loop(0, 8)
        def _(q):
            pltpu.make_async_copy(
                out_proj.at[:, pl.ds(pl.multiple_of(q * 896 + 384, 128), 128)],
                w.at[slot, q, :, pl.ds(0, 128)], w_sem.at[slot]).start()

    def w_wait(slot):
        arrived(w.at[slot], w_sem.at[slot])

    vup_copy = pltpu.make_async_copy(value_up, vup, vup_sem)
    vup_copy.start()
    lat_start(0, 0)
    lat_start(1, 1)
    w_start(0, 0)
    pl.semaphore_wait(barrier, 9)

    own = g * 4

    def block(yy, cc):
        return (yy * 2 + cc) * 4

    below, above, across = block(off(y, 3), core), block(off(y, 1), core), block(off(y, 2), core)

    class Gather:
        def __init__(self, kind, src, gathered):
            self.kind, self.src, self.all = kind, src, gathered

        def send(self, source, unit, count, sem, to):
            remote(source, self.all.at[pl.ds(unit, count)], y_send.at[self.kind], y_recv.at[self.kind, sem], to).start()

        def own(self, k):
            self.send(self.src.at[pl.ds(k, 1)], own + k, 1, min(k, 2), y_up)
            m = (k + 2) % 4
            self.send(self.src.at[pl.ds(m, 1)], own + m, 1, 4 + min(k, 2), y_down)

        def pass_on(self, k):
            self.wait(k, 1)
            self.send(self.all.at[pl.ds(below + k, 1)], below + k, 1, 3, y_up)
            self.wait(4 + k, 1)
            self.send(self.all.at[pl.ds(above + 2 + k, 1)], above + 2 + k, 1, 7, y_down)

        def share_own(self):
            self.send(self.src, own, 4, 8, sibling)

        def share_near(self):
            self.wait(2, 2)
            self.wait(6, 2)
            self.send(self.all.at[pl.ds(below, 4)], below, 4, 9, sibling)
            self.send(self.all.at[pl.ds(above, 4)], above, 4, 9, sibling)

        def share_far(self):
            self.wait(3, 2)
            self.wait(7, 2)
            self.send(self.all.at[pl.ds(across, 4)], across, 4, 10, sibling)

        def wait(self, sem, units):
            arrived(self.all.at[pl.ds(0, units)], y_recv.at[self.kind, sem])

        def wait_shared(self):
            self.wait(8, 4)
            self.wait(9, 8)
            self.wait(10, 4)

        def wait_sent(self):
            arrived(self.all.at[pl.ds(0, 28)], y_send.at[self.kind])

    dn = Gather(0, down, gdn)
    up = Gather(1, up_t, gup)

    def start(copies):
        for c in copies:
            c.start()

    dn.own(0)
    dn.own(1)
    own_dn = pltpu.make_async_copy(down, gdn.at[pl.ds(own, 4)], own_sem.at[0])
    own_up = pltpu.make_async_copy(up_t, gup.at[pl.ds(own, 4)], own_sem.at[1])

    vup_copy.wait()

    def heads_rows(c):
        slot = lax.rem(c, 2)
        arrived(lat.at[slot], lat_sem.at[slot])
        for k in range(4):
            wide[k] = lat[slot, k].astype(F32)

        @pl.when(c < 2)
        def _():
            lat_start(c + 2, slot)

        for h in range(8):
            xh = jnp.concatenate([wide[k, pl.ds(h, 256, stride=8), :] for k in range(4)], axis=1).astype(BF16)
            heads[pl.ds(pl.multiple_of(c * 256, 256), 256), pl.ds(h * 128, 128)] = jnp.dot(
                xh, vup[h], preferred_element_type=F32).astype(BF16)

    heads_rows(jnp.int32(0))
    heads_rows(jnp.int32(1))
    w_start(1, 1)

    coord = (x, z)
    ring = (x_at, z_at)

    def piece(c, dim, dest, half):
        slot = lax.rem(c // 2, P_SLOTS)
        rows = pl.ds(pl.multiple_of(lax.rem(c, 2) * 256 + dim * 128 + half * 64, 64), 64)
        return p.at[slot, dest, :, rows, :] if dim == 0 else p.at[slot, :, dest, rows, :]

    def s_copies(c, kind):
        slot, n1, n5 = lax.rem(c // 2, P_SLOTS), lax.rem(c, S1_SLOTS), lax.rem(c, S23_SLOTS)
        copies = []
        for dim in range(2):
            me, to = coord[dim], ring[dim]
            plus, opp, minus = off(me, 1), off(me, 2), off(me, 3)
            what = {0: ((opp, 0), (opp, 1)), 1: ((plus, 1), (minus, 0)), 2: ((plus, 0), (minus, 1))}[kind]
            land = (s1r.at[n1], s23r.at[n5, 0], s23r.at[n5, 1])[kind]
            sem = s1_recv.at[n1] if kind == 0 else s23_recv.at[n5]
            for way in range(2):
                dest, half = what[way]
                copies.append(remote(
                    piece(c, dim, dest, half), land.at[dim, way],
                    s_send.at[slot], sem, to[1] if way == 0 else to[3]))
        return copies

    def t_copies(c, kind):
        slot, n3, n5 = lax.rem(c, R_SLOTS), lax.rem(c, S1_SLOTS), lax.rem(c, S23_SLOTS)
        copies = []
        for dim in range(2):
            me, to = coord[1 - dim], ring[1 - dim]
            plus, opp, minus = off(me, 1), off(me, 2), off(me, 3)
            what = {0: ((opp, 0), (opp, 1)), 1: ((plus, 1), (minus, 0)), 2: ((plus, 0), (minus, 1))}[kind]
            land = (t1r.at[n3], t23r.at[n5, 0], t23r.at[n5, 1])[kind]
            sem = t1_recv.at[n3] if kind == 0 else t23_recv.at[n5]
            for way in range(2):
                dest, half = what[way]
                copies.append(remote(
                    r.at[slot, dim, dest, pl.ds(half * 64, 64), :], land.at[dim, way],
                    t_send.at[slot], sem, to[1] if way == 0 else to[3]))
        return copies

    def s_sent(slot):
        arrived(p.at[slot, pl.ds(0, 3)], s_send.at[slot])

    def produce(c):
        slot = lax.rem(c, P_SLOTS)

        @pl.when(c >= P_SLOTS)
        def _():
            s_sent(slot)

        @pl.when(c < 6)
        def _():
            wslot = lax.rem(c // 2, 2)

            @pl.when(lax.rem(c, 2) == 0)
            def _():
                w_wait(wslot)

            rows = pl.ds(pl.multiple_of(lax.rem(c, 2) * 512, 512), 512)

            @pl.loop(0, 8)
            def _(q):
                o = jnp.dot(heads[rows, :], w[wslot, q], preferred_element_type=F32).astype(BF16)
                p[slot, q // 2, lax.rem(q, 2) * 2] = o[:, :128]
                p[slot, q // 2, lax.rem(q, 2) * 2 + 1] = o[:, 128:]

            @pl.when(c == 1)
            def _():
                w_start(2, 0)

            @pl.when(c == 3)
            def _():
                w_start_tail(1)

        @pl.when(c == 6)
        def _():
            arrived(w.at[1, :, :, pl.ds(0, 128)], w_sem.at[1])
            lane = lax.broadcasted_iota(jnp.int32, (512, 128), 1)

            @pl.loop(0, 8)
            def _(q):
                wq = w[1, q, :, pl.ds(0, 128)]
                top = jnp.dot(heads[pl.ds(0, 512), :], wq, preferred_element_type=F32)
                bottom = jnp.dot(heads[pl.ds(512, 512), :], wq, preferred_element_type=F32)
                p[slot, q // 2, lax.rem(q, 2) * 2] = jnp.where(lane < 64, top, roll64(bottom)).astype(BF16)
                p[slot, q // 2, lax.rem(q, 2) * 2 + 1] = jnp.where(lane < 64, roll64(top), bottom).astype(BF16)

    def pass_on(c):
        n1 = lax.rem(c, S1_SLOTS)
        arrived(s1r.at[n1], s1_recv.at[n1])
        for dim in range(2):
            for way in range(2):
                dest = off(coord[dim], 1 if way == 0 else 3)
                ref = piece(c, dim, dest, way)
                ref[...] = (ref[...].astype(F32) + s1r[n1, dim, way].astype(F32)).astype(BF16)
        start(s_copies(c, 2))

    def reduce_first(c):
        n5, rs = lax.rem(c, S23_SLOTS), lax.rem(c, R_SLOTS)
        arrived(s23r.at[n5], s23_recv.at[n5])
        for dim in range(2):
            for half in range(2):
                mine = piece(c, dim, coord[dim], half)[...].astype(F32)
                total = mine + s23r[n5, 1, dim, half].astype(F32) + s23r[n5, 0, dim, 1 - half].astype(F32)
                r[rs, dim, :, pl.ds(half * 64, 64), :] = total.astype(BF16)
        start(t_copies(c, 0))
        start(t_copies(c, 1))

    def pass_on_second(c):
        rs, n3 = lax.rem(c, R_SLOTS), lax.rem(c, S1_SLOTS)
        arrived(t1r.at[n3], t1_recv.at[n3])
        for dim in range(2):
            for way in range(2):
                dest = off(coord[1 - dim], 1 if way == 0 else 3)
                ref = r.at[rs, dim, dest, pl.ds(way * 64, 64), :]
                ref[...] = (ref[...].astype(F32) + t1r[n3, dim, way].astype(F32)).astype(BF16)
        start(t_copies(c, 2))

    def reduce_second(c):
        rs, n5 = lax.rem(c, R_SLOTS), lax.rem(c, S23_SLOTS)
        arrived(t23r.at[n5], t23_recv.at[n5])
        for dim in range(2):
            for half in range(2):
                mine = r[rs, dim, coord[1 - dim], pl.ds(half * 64, 64), :].astype(F32)
                f[c, pl.ds(dim * 128 + half * 64, 64), :] = (
                    mine + t23r[n5, 1, dim, half].astype(F32) + t23r[n5, 0, dim, 1 - half].astype(F32))
        arrived(r.at[rs, :, pl.ds(0, 3)], t_send.at[rs])

    def l_copies(phase):
        copies = []
        for dim in range(2):
            me, to = coord[dim], ring[dim]
            other, to_other = coord[1 - dim], ring[1 - dim]
            mine = dim * 4 + me
            part = pl.ds(pl.multiple_of(other * 64, 64), 64)
            for k in range(1, 4):
                if phase == 0:
                    src, dst, dev = low.at[dim * 4 + off(me, k)], l1r.at[dim, k - 1], to[k]
                elif phase == 1:
                    src = mid.at[dim, pl.ds(pl.multiple_of(off(other, k) * 64, 64), 64), :]
                    dst, dev = l2r.at[dim, k - 1], to_other[k]
                elif phase == 2:
                    src = dst = lowf.at[mine, part, :]
                    dev = to_other[k]
                else:
                    src = dst = lowf.at[mine]
                    dev = to[k]
                copies.append(remote(src, dst, l_send.at[phase], l_recv.at[phase], dev))
        return copies

    def low_images():
        own_dn.wait()
        dn.wait_shared()

        @pl.loop(0, 8)
        def _(q):
            rows = pl.ds(pl.multiple_of((q // 2) * 256, 256), 256)
            chosen = gdn[ids[lax.rem(q, 2), q // 2]]
            low[q] = lax.dot_general(
                heads[rows, :], chosen, (((1,), (1,)), ((), ())), preferred_element_type=F32).astype(BF16)

        start(l_copies(0))

    def low_second():
        arrived(l1r, l_recv.at[0])
        for dim in range(2):
            total = low[dim * 4 + coord[dim]].astype(F32)
            for k in range(3):
                total = total + l1r[dim, k].astype(F32)
            mid[dim] = total.astype(BF16)
        start(l_copies(1))

    def low_third():
        arrived(l2r, l_recv.at[1])
        for dim in range(2):
            part = pl.ds(pl.multiple_of(coord[1 - dim] * 64, 64), 64)
            total = mid[dim, part, :].astype(F32)
            for k in range(3):
                total = total + l2r[dim, k].astype(F32)
            lowf[dim * 4 + coord[dim], part, :] = total.astype(BF16)
        start(l_copies(2))

    def low_fourth():
        arrived(l2r, l_recv.at[2])
        start(l_copies(3))

    @pl.loop(0, CHUNKS + 4 * LAG)
    def _(i):
        @pl.when((i < CHUNKS) & (lax.rem(i, 2) == 0))
        def _():
            produce(i // 2)

        @pl.when(i < CHUNKS)
        def _():
            start(s_copies(i, 0))
            start(s_copies(i, 1))

        for stage, work in enumerate((pass_on, reduce_first, pass_on_second, reduce_second)):
            behind = (stage + 1) * LAG
            pl.when((i >= behind) & (i < CHUNKS + behind))(functools.partial(work, i - behind))

        @pl.when(i < 2)
        def _():
            heads_rows(i + 2)

        @pl.when(i == 0)
        def _():
            own_dn.start()

        @pl.when(i == 1)
        def _():
            dn.own(2)
            dn.share_own()
            own_up.start()

        @pl.when(i == 2)
        def _():
            dn.own(3)

        @pl.when(i == 5)
        def _():
            dn.pass_on(0)

        @pl.when(i == 6)
        def _():
            dn.pass_on(1)

        @pl.when(i == 9)
        def _():
            dn.share_near()

        @pl.when(i == 10)
        def _():
            up.own(0)
            up.own(1)

        @pl.when(i == 11)
        def _():
            up.own(2)
            up.own(3)

        @pl.when(i == 13)
        def _():
            dn.share_far()
            up.share_own()

        @pl.when(i == 14)
        def _():
            low_images()

        @pl.when(i == 16)
        def _():
            low_second()
            up.pass_on(0)
            up.pass_on(1)

        @pl.when(i == 18)
        def _():
            low_third()

        @pl.when(i == 20)
        def _():
            low_fourth()
            up.share_near()

    up.share_far()
    own_up.wait()

    lane = lax.broadcasted_iota(jnp.int32, (256, 128), 1)
    for b in range(4):
        main = [f[4 * t + b] for t in range(3)]
        tail = f[12 + b % 2]
        if b >= 2:
            tail = roll64(tail)

        def keep(tiles):
            for t in range(4):
                wide[b, pl.ds(t * 256, 256), :] = tiles[t]

        @pl.when(lax.rem(z, 2) == 0)
        def _():
            keep(main + [tail])

        @pl.when(lax.rem(z, 2) == 1)
        def _():
            turned = [roll64(m) for m in main]
            keep([
                jnp.where(lane < 64, tail, turned[0]),
                jnp.where(lane < 64, turned[0], turned[1]),
                jnp.where(lane < 64, turned[1], turned[2]),
                turned[2],
            ])

        for k in range(2):
            wide[b, pl.ds(1024 + k * 256, 256), :] = jnp.broadcast_to(mix[k:k + 1, b * 256:(b + 1) * 256], (128, 256)).T

    arrived(lowf.at[pl.ds(0, 6)], l_recv.at[3])
    up.wait_shared()

    for b in range(4):
        rows = pl.ds(b * 256, 256)
        first, second = [
            lax.dot_general(
                lowf[b * 2 + k], gup[ids[k, b]], (((1,), (1,)), ((), ())),
                preferred_element_type=F32).astype(BF16).astype(F32)
            for k in range(2)
        ]
        w0, w1 = wide[b, pl.ds(1024, 256), :], wide[b, pl.ds(1280, 256), :]
        for t in range(4):
            n = 128 if t < 3 else 64
            cols = slice(t * 128, t * 128 + n)
            mixed = wide[b, pl.ds(t * 256, 256), :][:, :n] + (w0[:, :n] * first[:, cols] + w1[:, :n] * second[:, cols])
            staged[rows, pl.ds(t * 128, n)] = mixed.astype(BF16)
        pltpu.make_async_copy(staged.at[rows], out.at[rows], out_sem).start()

    for slot in range(P_SLOTS):
        s_sent(slot)
    arrived(staged, out_sem)
    dn.wait_sent()
    up.wait_sent()
    for phase, ref in enumerate((low.at[pl.ds(0, 6)], l2r, l2r, low.at[pl.ds(0, 6)])):
        arrived(ref, l_send.at[phase])


def local(latent, value_up, out_proj, adapter_down, adapter_up, pair_ids, mix_weights):
    rows = latent.shape[0]
    any_ = pl.BlockSpec(memory_space=pl.ANY)
    vmem = pl.BlockSpec(memory_space=pltpu.VMEM)
    smem = pl.BlockSpec(memory_space=pltpu.SMEM)
    dma = pltpu.SemaphoreType.DMA
    scratch = [
        pltpu.VMEM((2, 4, 2048, 128), BF16),
        pltpu.VMEM((4, 2048, 128), F32),
        pltpu.VMEM((8, 512, 128), BF16),
        pltpu.VMEM((rows, 1024), BF16),
        pltpu.VMEM((2, 8, 1024, 256), BF16),
        pltpu.VMEM((P_SLOTS, 4, 4, 512, 128), BF16),
        pltpu.VMEM((S1_SLOTS, 2, 2, 4, 64, 128), BF16),
        pltpu.VMEM((S23_SLOTS, 2, 2, 2, 4, 64, 128), BF16),
        pltpu.VMEM((R_SLOTS, 2, 4, 128, 128), BF16),
        pltpu.VMEM((S1_SLOTS, 2, 2, 64, 128), BF16),
        pltpu.VMEM((S23_SLOTS, 2, 2, 2, 64, 128), BF16),
        pltpu.VMEM((CHUNKS, 256, 128), F32),
        pltpu.VMEM((32, 256, 1024), BF16),
        pltpu.VMEM((32, 448, 256), BF16),
        pltpu.VMEM((8, 256, 256), BF16),
        pltpu.VMEM((2, 3, 256, 256), BF16),
        pltpu.VMEM((2, 256, 256), BF16),
        pltpu.VMEM((2, 3, 64, 256), BF16),
        pltpu.VMEM((8, 256, 256), BF16),
        pltpu.VMEM((rows, 448), BF16),
        dma((2,)), dma, dma((2,)), dma((2,)), dma,
        dma((P_SLOTS,)), dma((S1_SLOTS,)), dma((S23_SLOTS,)),
        dma((R_SLOTS,)), dma((S1_SLOTS,)), dma((S23_SLOTS,)),
        dma((2,)), dma((2, 11)), dma((4,)), dma((4,)),
    ]
    return pl.pallas_call(
        kernel,
        out_shape=jax.ShapeDtypeStruct((rows, adapter_up.shape[2]), BF16),
        in_specs=[any_, any_, any_, any_, any_, smem, vmem],
        out_specs=any_,
        scratch_shapes=scratch,
        compiler_params=pltpu.CompilerParams(
            collective_id=1, has_side_effects=True, vmem_limit_bytes=64 << 20),
        name="project",
    )(
        latent.reshape(rows * 8, 512), value_up, out_proj, adapter_down,
        jnp.swapaxes(adapter_up, 1, 2), pair_ids.T, mix_weights,
    )


def solution(mesh):
    placed = (
        P("grp", "dev", None),
        P("dev", None, None),
        P("dev", None),
        P("grp", None, "dev"),
        P("grp", None, "dev"),
        P("grp", None),
        P(None, "grp"),
    )
    return jax.shard_map(
        local, mesh=mesh, in_specs=placed, out_specs=P("grp", "dev"), check_vma=False
    )
```
